32 devices in a mesh: blk: 32 (over z, y, x, core), chan: 1.
Axes of the slice: x: 2, y: 2, z: 4, core: 2. Of those that a mesh axis runs over, the one named last changes fastest.
Arguments:
- spec_in: bfloat16 [256, 2, 512, 128], P('chan', None, 'blk'), may hold values from -6 to 6
- weight: bfloat16 [128, 2, 256, 256], P('blk', None, 'chan'), may hold values from -0.375 to 0.375
- pattern: int32 [128, 4, 4], P('blk'), may hold values 0 or 1
- cotangent: bfloat16 [256, 2, 512, 128], P('chan', None, 'blk'), may hold values from -6 to 6
Outputs:
- spec_out: bfloat16 [256, 2, 512, 128], P('chan', None, 'blk')
- grad_in: bfloat16 [256, 2, 512, 128], P('chan', None, 'blk')
- grad_weight: float32 [128, 2, 256, 256], P('blk', None, 'chan')
The draws below stay inside these ranges and needn't reach their ends.
All inputs are finite; a program needn't handle non-finite values. No bound on the sum of `pattern` on one device may be relied on, other than what follows from the above.
Results may differ from the reference program's by a relative error of at most 0.001.
Values may be sent and summed in bfloat16 or wider, within the bound.
No kernel may reach another device: no remote copies, remote signals or barrier semaphores. Data moves between devices by JAX's collectives and lax.ppermute only.
A program may use at most 256 MiB of HBM per device.

```python
import jax
import jax.numpy as jnp
from jax import lax

C = 256
BLOCK = 64
NB = 4
SAMPLES = 512
MODES = 128


def plant(entries, own_key, least, largest):
    longest = entries.shape.index(max(entries.shape))
    spots = []
    for shift in (0, 1):
        where = [jax.random.randint(jax.random.fold_in(own_key, axis), (), 0, length) for axis, length in enumerate(entries.shape)]
        where[longest] = (where[longest] + shift) % entries.shape[longest]
        spots.append(tuple(where))
    return entries.at[spots[0]].set(least).at[spots[1]].set(largest)


def spiked(result, own_key, source, target, parts, factor):
    owner, partner = [(jnp.arange(result.shape[dim]) // (result.shape[dim] // parts)).reshape([-1 if axis == dim else 1 for axis in range(result.ndim)]) for dim in (source, target)]
    chosen = jax.random.permutation(own_key, parts)[partner]
    strong = (owner == chosen) | (owner == (partner + parts // 2) % parts)
    return jnp.where(strong, factor * result, result)


def shard_levels(rng, shape, shards, least, largest):
    gain = 1.0
    for axis_at, shards_of in shards:
        draws = jax.random.uniform(jax.random.fold_in(jax.random.fold_in(rng, 6), axis_at), (shards_of,), jnp.float32, least / len(shards), largest / len(shards))
        gain = gain * jnp.repeat(jnp.exp(draws), shape[axis_at] // shards_of).reshape((-1,) + (1,) * (len(shape) - 1 - axis_at))
    return gain


def scatter_about(stream_key, shape, width, bound, cuts=(), held_as=jnp.bfloat16):
    entries = jax.random.normal(stream_key, shape, jnp.float32) * width
    if len(cuts) > 0:
        entries = shard_levels(stream_key, shape, cuts, -0.22, 0.18) * entries
    return jnp.clip(entries, min=-bound, max=bound).astype(held_as)


def noise_with(rng, dims, spread, limit, cuts, heavy, dtype=jnp.bfloat16):
    result = spread * jax.random.normal(rng, dims, jnp.float32)
    if cuts:
        result = result * shard_levels(rng, dims, cuts, -0.22, 0.18)
    return jnp.clip(spiked(result, jax.random.fold_in(rng, 3), *heavy), -limit, limit).astype(dtype)


def setup_inputs(seed: int = 0) -> dict:
    seeds = jax.random.split(jax.random.key(seed), 5)
    spec_in = noise_with(seeds[0], (C, 2, SAMPLES, MODES), 1.0, 6.0, ((2, 32),), (2, 3, 32, 2.75))
    weight = scatter_about(seeds[1], (MODES, 2, C, C), C ** -0.5, 0.375, ((0, 32),))
    pattern = plant((jax.random.randint(seeds[2], (MODES, NB, NB), 0, 2) < 1).astype(jnp.int32), jax.random.fold_in(seeds[2], 1), 0, 1)
    cotangent = noise_with(seeds[3], (C, 2, SAMPLES, MODES), 1.0, 6.0, ((2, 32),), (2, 3, 32, 2.75))
    return dict(spec_in=spec_in, weight=weight, pattern=pattern, cotangent=cotangent)


def expand_mask(pattern, block_size):
    rows = jnp.repeat(pattern.astype(jnp.float32), block_size, axis=1)
    return jnp.repeat(rows, block_size, axis=2)


def product(form, left, right):
    return jnp.einsum(form, left, right, precision=lax.Precision.HIGHEST)


def reference(spec_in, weight, pattern, cotangent):
    block_mask = expand_mask(pattern, BLOCK)
    masked = weight.astype(jnp.float32) * block_mask[:, None]
    inputs = spec_in.astype(jnp.float32)
    grads = cotangent.astype(jnp.float32)
    w_real = masked[:, 0]
    w_imag = masked[:, 1]

    form = "ism,mio->osm"
    out_real = product(form, inputs[:, 0], w_real) - product(form, inputs[:, 1], w_imag)
    out_imag = product(form, inputs[:, 0], w_imag) + product(form, inputs[:, 1], w_real)
    spec_out = jnp.stack([out_real, out_imag], axis=1).astype(jnp.bfloat16)

    back = "osm,mio->ism"
    dx_real = product(back, grads[:, 0], w_real) + product(back, grads[:, 1], w_imag)
    dx_imag = product(back, grads[:, 1], w_real) - product(back, grads[:, 0], w_imag)
    grad_in = jnp.stack([dx_real, dx_imag], axis=1).astype(jnp.bfloat16)

    outer = "ism,osm->mio"
    dw_real = product(outer, inputs[:, 0], grads[:, 0]) + product(outer, inputs[:, 1], grads[:, 1])
    dw_imag = product(outer, inputs[:, 0], grads[:, 1]) - product(outer, inputs[:, 1], grads[:, 0])
    grad_weight = jnp.stack([dw_real * block_mask, dw_imag * block_mask], axis=1)
    return spec_out, grad_in, grad_weight
```

```python
import jax
import jax.numpy as jnp
from jax import lax
from jax.experimental import pallas as pl
from jax.experimental.layout import Layout, with_layout_constraint
from jax.experimental.pallas import tpu as pltpu
from jax.sharding import PartitionSpec as P

F32 = jnp.float32
NN = (((1,), (0,)), ((), ()))
NT = (((1,), (1,)), ((), ()))
TN = (((0,), (0,)), ((), ()))


def dot(left, right, dims):
    return lax.dot_general(left, right, dims, preferred_element_type=F32)


def mix_kernel(x_ref, g_ref, w_ref, y_ref, d_ref):
    inner, samples = x_ref.shape[0], x_ref.shape[4]

    def products(ref, j, dims):
        rows = ref[:, 0, j].reshape(inner * 2 * samples, ref.shape[-1])
        for c in range(2):
            yield dot(rows, w_ref[0, j, c], dims).reshape(inner, 2, samples, -1)

    for j in range(w_ref.shape[1]):
        real, imag = products(x_ref, j, NN)
        y_ref[:, 0, j, 0] = (real[:, 0] - imag[:, 1]).astype(y_ref.dtype)
        y_ref[:, 0, j, 1] = (real[:, 1] + imag[:, 0]).astype(y_ref.dtype)
        real, imag = products(g_ref, j, NT)
        d_ref[:, 0, j, 0] = (real[:, 0] + imag[:, 1]).astype(d_ref.dtype)
        d_ref[:, 0, j, 1] = (real[:, 1] - imag[:, 0]).astype(d_ref.dtype)


def mix(x, g, w, y_type):
    inner, outer, modes, _, samples, _ = x.shape
    ci, co = w.shape[3:]
    some = 2 if modes % 2 == 0 else 1

    def block(channels):
        return pl.BlockSpec((inner, 1, some, 2, samples, channels), lambda z, j: (0, z, j, 0, 0, 0))

    return pl.pallas_call(
        mix_kernel,
        grid=(outer, modes // some),
        in_specs=[block(ci), block(co), pl.BlockSpec((1, some, 2, ci, co), lambda z, j: (z, j, 0, 0, 0))],
        out_specs=[block(co), block(ci)],
        out_shape=[
            jax.ShapeDtypeStruct(x.shape[:-1] + (co,), y_type),
            jax.ShapeDtypeStruct(x.shape[:-1] + (ci,), jnp.bfloat16),
        ],
        compiler_params=pltpu.CompilerParams(vmem_limit_bytes=32 * 1024 * 1024),
        name="mix",
    )(x, g, w)


def weight_grad_kernel(layer_ref, x_ref, g_ref, *refs):
    *both_refs, mask_ref, out_ref = refs
    ci = x_ref.shape[-1]

    def rows(ref, c):
        return ref[..., c, :, :].reshape(-1, ref.shape[-1])

    def add(x_real, x_imag, g_real, g_imag):
        out_ref[0, 0] += dot(x_real, g_real, TN) + dot(x_imag, g_imag, TN)
        out_ref[0, 1] += dot(x_real, g_imag, TN) - dot(x_imag, g_real, TN)

    out_ref[...] = jnp.zeros_like(out_ref)
    add(rows(x_ref, 0), rows(x_ref, 1), rows(g_ref, 0), rows(g_ref, 1))
    for ref in both_refs:
        real, imag = rows(ref, 0), rows(ref, 1)
        add(real[:, :ci], imag[:, :ci], real[:, ci:], imag[:, ci:])
    out_ref[0] *= mask_ref[...].astype(F32)


def weight_grad(layer, x, g, both, mask):
    inner, _, modes, _, samples, ci = x.shape
    co = g.shape[-1]

    def own(channels):
        return pl.BlockSpec((inner, 1, 1, 2, samples, channels), lambda j, layer: (0, layer[0], j, 0, 0, 0))

    return pl.pallas_call(
        weight_grad_kernel,
        grid_spec=pltpu.PrefetchScalarGridSpec(
            num_scalar_prefetch=1,
            grid=(modes,),
            in_specs=[
                own(ci),
                own(co),
                *[pl.BlockSpec((inner, 1, 2, samples, ci + co), lambda j, layer: (0, j, 0, 0, 0))] * len(both),
                pl.BlockSpec((1, ci, co), lambda j, layer: (j, 0, 0)),
            ],
            out_specs=pl.BlockSpec((1, 2, ci, co), lambda j, layer: (j, 0, 0, 0)),
        ),
        out_shape=jax.ShapeDtypeStruct((modes, 2, ci, co), F32),
        compiler_params=pltpu.CompilerParams(vmem_limit_bytes=32 * 1024 * 1024),
        name="weight_grad",
    )(layer, x, g, *both, mask)


def stage(ready, work, *operands):
    shapes = jax.eval_shape(work, *operands)
    return lax.cond(ready, work, lambda *_: jax.tree.map(lambda a: jnp.zeros(a.shape, a.dtype), shapes), *operands)


def local(spec_in, weight, pattern, cotangent):
    ranks = lax.axis_size("blk")
    chans = lax.axis_size("chan")
    outer = 4 if ranks % 4 == 0 else 1
    inner = ranks // outer
    layer = lax.axis_index("blk") // inner
    layers = [[z * inner + r for r in range(inner)] for z in range(outer)]
    columns = [[z * inner + r for z in range(outer)] for r in range(inner)]
    modes = weight.shape[0]
    in_rows, width = weight.shape[2:]
    block_size = width // pattern.shape[2]

    mask = jnp.repeat(jnp.repeat(pattern.astype(jnp.bfloat16), block_size, axis=1), block_size, axis=2)
    own_mask = lax.dynamic_slice_in_dim(mask, lax.axis_index("chan") * in_rows, in_rows, 1)
    masked = weight * own_mask[:, None]
    held = lax.all_gather(masked, "blk", axis=0, axis_index_groups=columns)

    def exchange(a):
        return lax.all_to_all(a, "blk", 0, 0, tiled=True, axis_index_groups=layers)

    def to_modes(a):
        turned = a.transpose(3, 1, 2, 0)
        return turned.reshape(outer, inner, modes, *turned.shape[1:]).swapaxes(0, 1)

    def to_samples(a):
        turned = a.swapaxes(0, 1)
        return turned.reshape(ranks * modes, *turned.shape[3:]).transpose(3, 1, 2, 0)

    def to_owners(x, g):
        pieces = []
        for step in range(1, outer):
            parts = [lax.dynamic_index_in_dim(a, layer ^ step, 1, keepdims=False) for a in (x, g)]
            both = jnp.concatenate(parts, axis=-1)
            pieces.append(lax.ppermute(both, "blk", [(i, i ^ (step * inner)) for i in range(ranks)]))
        return pieces

    def inward(x, g):
        return exchange(to_modes(x)), exchange(to_modes(g))

    def outward(x, g, held):
        y, d = mix(x, g, held, jnp.bfloat16 if chans == 1 else F32)
        if chans > 1:
            y = lax.psum_scatter(y, "chan", scatter_dimension=5, tiled=True).astype(jnp.bfloat16)
        y, d = exchange(y), exchange(d)
        return tuple(with_layout_constraint(to_samples(a), Layout((0, 1, 2, 3))) for a in (y, d))

    ready = pattern[0, 0, 0] < 2
    if chans > 1:
        cotangent = lax.all_gather(cotangent, "chan", axis=0, tiled=True)
    x, g = stage(ready, inward, spec_in, cotangent)
    owned = to_owners(x, g)
    spec_out, grad_in = stage(ready, outward, x, g, held)
    spec_out, grad_in, owned = lax.optimization_barrier((spec_out, grad_in, owned))
    grad_weight = weight_grad(layer.astype(jnp.int32).reshape(1), x, g, owned, own_mask)
    return spec_out, grad_in, grad_weight


def solution(mesh):
    in_specs = (
        P("chan", None, "blk", None),
        P("blk", None, "chan", None),
        P("blk", None, None),
        P("chan", None, "blk", None),
    )
    out_specs = (
        P("chan", None, "blk", None),
        P("chan", None, "blk", None),
        P("blk", None, "chan", None),
    )
    return jax.shard_map(local, mesh=mesh, in_specs=in_specs, out_specs=out_specs, check_vma=False)
```

```python
import functools

import jax
import jax.numpy as jnp
from jax import lax
from jax.experimental import pallas as pl
from jax.experimental.layout import Layout, with_layout_constraint
from jax.experimental.pallas import tpu as pltpu
from jax.sharding import PartitionSpec as P

F32 = jnp.float32
NN = (((1,), (0,)), ((), ()))
NT = (((1,), (1,)), ((), ()))
TN = (((0,), (0,)), ((), ()))


def dot(left, right, dims):
    return lax.dot_general(left, right, dims, preferred_element_type=F32)


def mix_kernel(layer_ref, x_ref, g_ref, *refs):
    *w_refs, y_ref, d_ref = refs
    inner, samples = x_ref.shape[0], x_ref.shape[4]

    def run(w_ref):
        def products(ref, j, dims):
            rows = ref[:, 0, j].reshape(inner * 2 * samples, ref.shape[-1])
            for c in range(2):
                yield dot(rows, w_ref[j, c], dims).reshape(inner, 2, samples, -1)

        for j in range(w_ref.shape[0]):
            real, imag = products(x_ref, j, NN)
            y_ref[:, 0, j, 0] = (real[:, 0] - imag[:, 1]).astype(y_ref.dtype)
            y_ref[:, 0, j, 1] = (real[:, 1] + imag[:, 0]).astype(y_ref.dtype)
            real, imag = products(g_ref, j, NT)
            d_ref[:, 0, j, 0] = (real[:, 0] + imag[:, 1]).astype(d_ref.dtype)
            d_ref[:, 0, j, 1] = (real[:, 1] - imag[:, 0]).astype(d_ref.dtype)

    for p, w_ref in enumerate(w_refs):
        pl.when(pl.program_id(0) == p)(functools.partial(run, w_ref))


def mix(layer, odd, x, g, ws, y_type):
    inner, outer, modes, _, samples, _ = x.shape
    ci, co = ws[0].shape[2:]
    some = 2 if modes % 2 == 0 else 1

    def block(channels):
        return pl.BlockSpec(
            (inner, 1, some, 2, samples, channels), lambda p, k, layer: (0, layer[0] ^ (odd + 2 * p), k, 0, 0, 0)
        )

    def result(channels):
        return pl.BlockSpec((inner, 1, some, 2, samples, channels), lambda p, k, layer: (0, (layer[0] // 2) ^ p, k, 0, 0, 0))

    def weights(own):
        rest = 0 if own else modes // some - 1
        return pl.BlockSpec((some, 2, ci, co), lambda p, k, layer: (jnp.where(p == own, k, rest), 0, 0, 0))

    return pl.pallas_call(
        mix_kernel,
        grid_spec=pltpu.PrefetchScalarGridSpec(
            num_scalar_prefetch=1,
            grid=(2, modes // some),
            in_specs=[block(ci), block(co), weights(0), weights(1)],
            out_specs=[result(co), result(ci)],
        ),
        out_shape=[
            jax.ShapeDtypeStruct((inner, 2, modes, 2, samples, co), y_type),
            jax.ShapeDtypeStruct((inner, 2, modes, 2, samples, ci), jnp.bfloat16),
        ],
        compiler_params=pltpu.CompilerParams(vmem_limit_bytes=40 * 1024 * 1024),
        name="mix",
    )(layer, x, g, *ws)


def weight_grad_kernel(layer_ref, x_ref, g_ref, *refs):
    *both_refs, mask_ref, out_ref = refs
    ci = x_ref.shape[-1]

    def rows(ref, c):
        return ref[..., c, :, :].reshape(-1, ref.shape[-1])

    def add(x_real, x_imag, g_real, g_imag):
        out_ref[0, 0] += dot(x_real, g_real, TN) + dot(x_imag, g_imag, TN)
        out_ref[0, 1] += dot(x_real, g_imag, TN) - dot(x_imag, g_real, TN)

    out_ref[...] = jnp.zeros_like(out_ref)
    add(rows(x_ref, 0), rows(x_ref, 1), rows(g_ref, 0), rows(g_ref, 1))
    for ref in both_refs:
        real, imag = rows(ref, 0), rows(ref, 1)
        add(real[:, :ci], imag[:, :ci], real[:, ci:], imag[:, ci:])
    out_ref[0] *= mask_ref[...].astype(F32)


def weight_grad(layer, x, g, both, mask):
    inner, _, modes, _, samples, ci = x.shape
    co = g.shape[-1]

    def own(channels):
        return pl.BlockSpec((inner, 1, 1, 2, samples, channels), lambda j, layer: (0, layer[0], j, 0, 0, 0))

    return pl.pallas_call(
        weight_grad_kernel,
        grid_spec=pltpu.PrefetchScalarGridSpec(
            num_scalar_prefetch=1,
            grid=(modes,),
            in_specs=[
                own(ci),
                own(co),
                *[pl.BlockSpec((inner, 1, 2, samples, ci + co), lambda j, layer: (0, j, 0, 0, 0))] * len(both),
                pl.BlockSpec((1, ci, co), lambda j, layer: (j, 0, 0)),
            ],
            out_specs=pl.BlockSpec((1, 2, ci, co), lambda j, layer: (j, 0, 0, 0)),
        ),
        out_shape=jax.ShapeDtypeStruct((modes, 2, ci, co), F32),
        compiler_params=pltpu.CompilerParams(vmem_limit_bytes=32 * 1024 * 1024),
        name="weight_grad",
    )(layer, x, g, *both, mask)


def stage(ready, work, *operands):
    shapes = jax.eval_shape(work, *operands)
    return lax.cond(ready, work, lambda *_: jax.tree.map(lambda a: jnp.zeros(a.shape, a.dtype), shapes), *operands)


def local(spec_in, weight, pattern, cotangent):
    ranks = lax.axis_size("blk")
    chans = lax.axis_size("chan")
    outer = 4
    inner = ranks // outer
    layer = lax.axis_index("blk") // inner
    layers = [[z * inner + r for r in range(inner)] for z in range(outer)]
    modes = weight.shape[0]
    in_rows, width = weight.shape[2:]
    block_size = width // pattern.shape[2]

    mask = jnp.repeat(jnp.repeat(pattern.astype(jnp.bfloat16), block_size, axis=1), block_size, axis=2)
    own_mask = lax.dynamic_slice_in_dim(mask, lax.axis_index("chan") * in_rows, in_rows, 1)
    masked = weight * own_mask[:, None]

    def exchange(a):
        return lax.all_to_all(a, "blk", 0, 0, tiled=True, axis_index_groups=layers)

    def to_modes(a):
        turned = a.transpose(3, 1, 2, 0)
        return turned.reshape(outer, inner, modes, *turned.shape[1:]).swapaxes(0, 1)

    def to_samples(same, other):
        even = layer % 2 == 0
        parts = jnp.where(even, same, other), jnp.where(even, other, same)
        turned = jnp.stack(parts, axis=2).transpose(1, 2, 0, *range(3, 7))
        turned = turned.reshape(ranks * modes, *turned.shape[4:]).transpose(3, 1, 2, 0)
        return with_layout_constraint(turned, Layout((0, 1, 2, 3)))

    def send(a, step):
        return lax.ppermute(a, "blk", [(i, i ^ (step * inner)) for i in range(ranks)])

    def for_owner(step):
        parts = [lax.dynamic_index_in_dim(a, layer ^ step, 1, keepdims=False) for a in (x, g)]
        return send(jnp.concatenate(parts, axis=-1), step)

    def mixed(odd, x, g, ws):
        y, d = mix(place, odd, x, g, ws, jnp.bfloat16 if chans == 1 else F32)
        if chans > 1:
            y = lax.psum_scatter(y, "chan", scatter_dimension=5, tiled=True).astype(jnp.bfloat16)
        return exchange(y), exchange(d)

    def outward(x, g, ws, y_same, d_same):
        y, d = mixed(1, x, g, ws)
        return to_samples(y_same, y), to_samples(d_same, d)

    barrier = lax.optimization_barrier
    place = layer.astype(jnp.int32).reshape(1)
    ready = pattern[0, 0, 0] < 2
    far, near = send(masked, 2), send(masked, 1)
    if chans > 1:
        cotangent = lax.all_gather(cotangent, "chan", axis=0, tiled=True)
    x, g = stage(ready, lambda a, b: (exchange(to_modes(a)), exchange(to_modes(b))), spec_in, cotangent)
    x, g, far, near = barrier((x, g, far, near))
    near_far = send(far, 1)
    owned = {step: for_owner(step) for step in (2, 3, 1)}
    y_same, d_same = stage(ready, functools.partial(mixed, 0), x, g, [masked, far])
    y_same, d_same, near_far = barrier((y_same, d_same, near_far))
    far_pairs = [near, near_far]
    spec_out, grad_in = stage(ready, outward, x, g, far_pairs, y_same, d_same)
    spec_out, grad_in, owned = barrier((spec_out, grad_in, owned))
    grad_weight = weight_grad(place, x, g, [owned[step] for step in (1, 2, 3)], own_mask)
    return spec_out, grad_in, grad_weight


def solution(mesh):
    in_specs = (
        P("chan", None, "blk", None),
        P("blk", None, "chan", None),
        P("blk", None, None),
        P("chan", None, "blk", None),
    )
    out_specs = (
        P("chan", None, "blk", None),
        P("chan", None, "blk", None),
        P("blk", None, "chan", None),
    )
    return jax.shard_map(local, mesh=mesh, in_specs=in_specs, out_specs=out_specs, check_vma=False)
```

```python
import functools

import jax
import jax.numpy as jnp
from jax import lax
from jax.experimental import pallas as pl
from jax.experimental.layout import Layout, with_layout_constraint
from jax.experimental.pallas import tpu as pltpu
from jax.sharding import PartitionSpec as P

F32 = jnp.float32
NN = (((1,), (0,)), ((), ()))
NT = (((1,), (1,)), ((), ()))
TN = (((0,), (0,)), ((), ()))


def dot(left, right, dims):
    return lax.dot_general(left, right, dims, preferred_element_type=F32)


def mix_kernel(layer_ref, x_ref, g_ref, same_ref, other_ref, *out_refs):
    inner, samples = x_ref.shape[0], x_ref.shape[4]
    y_ref, d_ref = out_refs if len(out_refs) == 2 else (out_refs[0].at[:, k] for k in range(2))

    def run(w_ref):
        def products(ref, j, dims):
            rows = ref[:, 0, j].reshape(inner * 2 * samples, ref.shape[-1])
            for c in range(2):
                yield dot(rows, w_ref[j, c], dims).reshape(inner, 2, samples, -1)

        for j in range(w_ref.shape[0]):
            real, imag = products(x_ref, j, NN)
            y_ref[:, 0, j, 0] = (real[:, 0] - imag[:, 1]).astype(y_ref.dtype)
            y_ref[:, 0, j, 1] = (real[:, 1] + imag[:, 0]).astype(y_ref.dtype)
            real, imag = products(g_ref, j, NT)
            d_ref[:, 0, j, 0] = (real[:, 0] + imag[:, 1]).astype(d_ref.dtype)
            d_ref[:, 0, j, 1] = (real[:, 1] - imag[:, 0]).astype(d_ref.dtype)

    for p, w_ref in enumerate((same_ref, other_ref)):
        pl.when(pl.program_id(0) == p)(functools.partial(run, w_ref))


def mix(layer, odd, x, g, ws, y_type, joint):
    inner, outer, modes, _, samples, _ = x.shape
    ci, co = ws[0].shape[2:]
    some = 2 if modes % 2 == 0 else 1

    def block(channels):
        return pl.BlockSpec(
            (inner, 1, some, 2, samples, channels), lambda p, k, layer: (0, layer[0] ^ (odd + 2 * p), k, 0, 0, 0)
        )

    def result(channels):
        return pl.BlockSpec((inner, 1, some, 2, samples, channels), lambda p, k, layer: (0, (layer[0] // 2) ^ p, k, 0, 0, 0))

    def weights(own):
        rest = 0 if own else modes // some - 1
        return pl.BlockSpec((some, 2, ci, co), lambda p, k, layer: (jnp.where(p == own, k, rest), 0, 0, 0))

    if joint:
        out_specs = [
            pl.BlockSpec((inner, 2, 1, some, 2, samples, co), lambda p, k, layer: (0, 0, (layer[0] // 2) ^ p, k, 0, 0, 0))
        ]
        out_shape = [jax.ShapeDtypeStruct((inner, 2, 2, modes, 2, samples, co), y_type)]
    else:
        out_specs = [result(co), result(ci)]
        out_shape = [
            jax.ShapeDtypeStruct((inner, 2, modes, 2, samples, co), y_type),
            jax.ShapeDtypeStruct((inner, 2, modes, 2, samples, ci), jnp.bfloat16),
        ]
    return pl.pallas_call(
        mix_kernel,
        grid_spec=pltpu.PrefetchScalarGridSpec(
            num_scalar_prefetch=1,
            grid=(2, modes // some),
            in_specs=[block(ci), block(co), weights(0), weights(1)],
            out_specs=out_specs,
        ),
        out_shape=out_shape,
        compiler_params=pltpu.CompilerParams(vmem_limit_bytes=40 * 1024 * 1024),
        name="mix",
    )(layer, x, g, *ws)


def weight_grad_kernel(layer_ref, *refs):
    *pairs, mask_ref, out_ref = refs

    def rows(ref, c):
        return ref[..., c, :, :].reshape(-1, ref.shape[-1])

    real = imag = 0.0
    for x_ref, g_ref in zip(pairs[::2], pairs[1::2]):
        x_real, x_imag, g_real, g_imag = rows(x_ref, 0), rows(x_ref, 1), rows(g_ref, 0), rows(g_ref, 1)
        real = real + dot(x_real, g_real, TN) + dot(x_imag, g_imag, TN)
        imag = imag + dot(x_real, g_imag, TN) - dot(x_imag, g_real, TN)
    mask = mask_ref[0].astype(F32)
    out_ref[0, 0] = real * mask
    out_ref[0, 1] = imag * mask


def weight_grad(layer, x, g, pairs, mask):
    inner, _, modes, _, samples, ci = x.shape
    co = g.shape[-1]

    def own(channels):
        return pl.BlockSpec((inner, 1, 1, 2, samples, channels), lambda j, layer: (0, layer[0], j, 0, 0, 0))

    def block(channels):
        return pl.BlockSpec((inner, 1, 2, samples, channels), lambda j, layer: (0, j, 0, 0, 0))

    return pl.pallas_call(
        weight_grad_kernel,
        grid_spec=pltpu.PrefetchScalarGridSpec(
            num_scalar_prefetch=1,
            grid=(modes,),
            in_specs=[own(ci), own(co), *[block(ci), block(co)] * len(pairs), pl.BlockSpec((1, ci, co), lambda j, layer: (j, 0, 0))],
            out_specs=pl.BlockSpec((1, 2, ci, co), lambda j, layer: (j, 0, 0, 0)),
        ),
        out_shape=jax.ShapeDtypeStruct((modes, 2, ci, co), F32),
        compiler_params=pltpu.CompilerParams(vmem_limit_bytes=40 * 1024 * 1024),
        name="weight_grad",
    )(layer, x, g, *(a for pair in pairs for a in pair), mask)


def stage(ready, work, *operands):
    shapes = jax.eval_shape(work, *operands)
    return lax.cond(ready, work, lambda *_: jax.tree.map(lambda a: jnp.zeros(a.shape, a.dtype), shapes), *operands)


def local(spec_in, weight, pattern, cotangent):
    ranks = lax.axis_size("blk")
    chans = lax.axis_size("chan")
    outer = 4
    inner = ranks // outer
    layer = lax.axis_index("blk") // inner
    layers = [[z * inner + r for r in range(inner)] for z in range(outer)]
    modes = weight.shape[0]
    in_rows, width = weight.shape[2:]
    block_size = width // pattern.shape[2]

    mask = jnp.repeat(jnp.repeat(pattern.astype(jnp.bfloat16), block_size, axis=1), block_size, axis=2)
    own_mask = lax.dynamic_slice_in_dim(mask, lax.axis_index("chan") * in_rows, in_rows, 1)
    masked = weight * own_mask[:, None]

    def exchange(a):
        return lax.all_to_all(a, "blk", 0, 0, tiled=True, axis_index_groups=layers)

    def to_modes(a):
        turned = a.transpose(3, 1, 2, 0)
        return turned.reshape(outer, inner, modes, *turned.shape[1:]).swapaxes(0, 1)

    def to_samples(same, other):
        even = layer % 2 == 0
        parts = jnp.where(even, same, other), jnp.where(even, other, same)
        turned = jnp.stack(parts, axis=2).transpose(1, 2, 0, *range(3, 7))
        turned = turned.reshape(ranks * modes, *turned.shape[4:]).transpose(3, 1, 2, 0)
        return with_layout_constraint(turned, Layout((0, 1, 2, 3)))

    def send(a, step):
        return lax.ppermute(a, "blk", [(i, i ^ (step * inner)) for i in range(ranks)])

    def for_owner(a, step):
        return send(lax.dynamic_index_in_dim(a, layer ^ step, 1, keepdims=False), step)

    def mixed(odd, joint, x, g, ws):
        out = list(mix(place, odd, x, g, ws, jnp.bfloat16 if chans == 1 else F32, joint))
        if chans > 1:
            out[0] = lax.psum_scatter(out[0], "chan", scatter_dimension=5, tiled=True).astype(jnp.bfloat16)
        return [exchange(a) for a in out]

    def outward(x, g, ws, same):
        y, d = mixed(1, False, x, g, ws)
        spec_out = to_samples(same[0][:, 0] if chans == 1 else same[0], y)
        same, d, spec_out = lax.optimization_barrier((same, d, spec_out))
        return spec_out, to_samples(same[0][:, 1] if chans == 1 else same[1], d)

    barrier = lax.optimization_barrier
    place = layer.astype(jnp.int32).reshape(1)
    ready = lax.axis_index("blk") < ranks
    far, near = send(masked, 2), send(masked, 1)
    if chans > 1:
        cotangent = lax.all_gather(cotangent, "chan", axis=0, tiled=True)
    x, turned = stage(ready, lambda a, b: (exchange(to_modes(a)), to_modes(b)), spec_in, cotangent)
    g = exchange(turned)
    x, far, near = barrier((x, far, near))
    near_far = send(far, 1)
    pairs = {step: [for_owner(x, step)] for step in (2, 3)}
    g, near = barrier((g, near))
    for step in (2, 3):
        pairs[step].append(for_owner(g, step))
    same = stage(ready, functools.partial(mixed, 0, chans == 1), x, g, [masked, far])
    same, near_far = barrier((same, near_far))
    x_late, g_late, near_far = barrier((x, g, near_far))
    pairs[1] = [for_owner(x_late, 1), for_owner(g_late, 1)]
    spec_out, grad_in = stage(ready, outward, x, g, [near, near_far], same)
    spec_out, grad_in, pairs = barrier((spec_out, grad_in, pairs))
    grad_weight = weight_grad(place, x, g, [pairs[step] for step in (1, 2, 3)], own_mask)
    return spec_out, grad_in, grad_weight


def solution(mesh):
    in_specs = (
        P("chan", None, "blk", None),
        P("blk", None, "chan", None),
        P("blk", None, None),
        P("chan", None, "blk", None),
    )
    out_specs = (
        P("chan", None, "blk", None),
        P("chan", None, "blk", None),
        P("blk", None, "chan", None),
    )
    return jax.shard_map(local, mesh=mesh, in_specs=in_specs, out_specs=out_specs, check_vma=False)
```

```python
import functools

import jax
import jax.numpy as jnp
from jax import lax
from jax.experimental import pallas as pl
from jax.experimental.layout import Layout, with_layout_constraint
from jax.experimental.pallas import tpu as pltpu
from jax.sharding import PartitionSpec as P

F32 = jnp.float32
NN = (((1,), (0,)), ((), ()))
NT = (((1,), (1,)), ((), ()))
TN = (((0,), (0,)), ((), ()))


def dot(left, right, dims):
    return lax.dot_general(left, right, dims, preferred_element_type=F32)


def mix_kernel(layer_ref, x_ref, g_ref, same_ref, other_ref, *out_refs):
    inner, samples = x_ref.shape[0], x_ref.shape[4]
    y_ref, d_ref = out_refs if len(out_refs) == 2 else (out_refs[0].at[:, k] for k in range(2))

    def run(w_ref):
        def products(ref, j, dims):
            rows = ref[:, 0, j].reshape(inner * 2 * samples, ref.shape[-1])
            for c in range(2):
                yield dot(rows, w_ref[j, c], dims).reshape(inner, 2, samples, -1)

        for j in range(w_ref.shape[0]):
            real, imag = products(x_ref, j, NN)
            y_ref[:, 0, j, 0] = (real[:, 0] - imag[:, 1]).astype(y_ref.dtype)
            y_ref[:, 0, j, 1] = (real[:, 1] + imag[:, 0]).astype(y_ref.dtype)
            real, imag = products(g_ref, j, NT)
            d_ref[:, 0, j, 0] = (real[:, 0] + imag[:, 1]).astype(d_ref.dtype)
            d_ref[:, 0, j, 1] = (real[:, 1] - imag[:, 0]).astype(d_ref.dtype)

    for p, w_ref in enumerate((same_ref, other_ref)):
        pl.when(pl.program_id(0) == p)(functools.partial(run, w_ref))


def mix(layer, odd, x, g, ws, y_type, joint):
    inner, outer, modes, _, samples, _ = x.shape
    ci, co = ws[0].shape[2:]
    some = 2 if modes % 2 == 0 else 1

    def block(channels):
        return pl.BlockSpec(
            (inner, 1, some, 2, samples, channels), lambda p, k, layer: (0, layer[0] ^ (odd + 2 * p), k, 0, 0, 0)
        )

    def result(channels):
        return pl.BlockSpec((inner, 1, some, 2, samples, channels), lambda p, k, layer: (0, (layer[0] // 2) ^ p, k, 0, 0, 0))

    def weights(own):
        rest = 0 if own else modes // some - 1
        return pl.BlockSpec((some, 2, ci, co), lambda p, k, layer: (jnp.where(p == own, k, rest), 0, 0, 0))

    if joint:
        out_specs = [
            pl.BlockSpec((inner, 2, 1, some, 2, samples, co), lambda p, k, layer: (0, 0, (layer[0] // 2) ^ p, k, 0, 0, 0))
        ]
        out_shape = [jax.ShapeDtypeStruct((inner, 2, 2, modes, 2, samples, co), y_type)]
    else:
        out_specs = [result(co), result(ci)]
        out_shape = [
            jax.ShapeDtypeStruct((inner, 2, modes, 2, samples, co), y_type),
            jax.ShapeDtypeStruct((inner, 2, modes, 2, samples, ci), jnp.bfloat16),
        ]
    return pl.pallas_call(
        mix_kernel,
        grid_spec=pltpu.PrefetchScalarGridSpec(
            num_scalar_prefetch=1,
            grid=(2, modes // some),
            in_specs=[block(ci), block(co), weights(0), weights(1)],
            out_specs=out_specs,
        ),
        out_shape=out_shape,
        compiler_params=pltpu.CompilerParams(vmem_limit_bytes=40 * 1024 * 1024),
        name="mix",
    )(layer, x, g, *ws)


def weight_grad_kernel(layer_ref, *refs):
    *pairs, mask_ref, out_ref = refs

    def rows(ref, c):
        return ref[..., c, :, :].reshape(-1, ref.shape[-1])

    real = imag = 0.0
    for x_ref, g_ref in zip(pairs[::2], pairs[1::2]):
        x_real, x_imag, g_real, g_imag = rows(x_ref, 0), rows(x_ref, 1), rows(g_ref, 0), rows(g_ref, 1)
        real = real + dot(x_real, g_real, TN) + dot(x_imag, g_imag, TN)
        imag = imag + dot(x_real, g_imag, TN) - dot(x_imag, g_real, TN)
    mask = mask_ref[0].astype(F32)
    out_ref[0, 0] = real * mask
    out_ref[0, 1] = imag * mask


def weight_grad(layer, x, g, pairs, mask):
    inner, _, modes, _, samples, ci = x.shape
    co = g.shape[-1]

    def own(channels):
        return pl.BlockSpec((inner, 1, 1, 2, samples, channels), lambda j, layer: (0, layer[0], j, 0, 0, 0))

    def block(channels):
        return pl.BlockSpec((inner, 1, 2, samples, channels), lambda j, layer: (0, j, 0, 0, 0))

    return pl.pallas_call(
        weight_grad_kernel,
        grid_spec=pltpu.PrefetchScalarGridSpec(
            num_scalar_prefetch=1,
            grid=(modes,),
            in_specs=[own(ci), own(co), *[block(ci), block(co)] * len(pairs), pl.BlockSpec((1, ci, co), lambda j, layer: (j, 0, 0))],
            out_specs=pl.BlockSpec((1, 2, ci, co), lambda j, layer: (j, 0, 0, 0)),
        ),
        out_shape=jax.ShapeDtypeStruct((modes, 2, ci, co), F32),
        compiler_params=pltpu.CompilerParams(vmem_limit_bytes=40 * 1024 * 1024),
        name="weight_grad",
    )(layer, x, g, *(a for pair in pairs for a in pair), mask)


def stage(ready, work, *operands):
    shapes = jax.eval_shape(work, *operands)
    return lax.cond(ready, work, lambda *_: jax.tree.map(lambda a: jnp.zeros(a.shape, a.dtype), shapes), *operands)


def local(spec_in, weight, pattern, cotangent):
    ranks = lax.axis_size("blk")
    chans = lax.axis_size("chan")
    outer = 4
    inner = ranks // outer
    layer = lax.axis_index("blk") // inner
    layers = [[z * inner + r for r in range(inner)] for z in range(outer)]
    modes = weight.shape[0]
    in_rows, width = weight.shape[2:]
    block_size = width // pattern.shape[2]

    mask = jnp.repeat(jnp.repeat(pattern.astype(jnp.bfloat16), block_size, axis=1), block_size, axis=2)
    own_mask = lax.dynamic_slice_in_dim(mask, lax.axis_index("chan") * in_rows, in_rows, 1)
    masked = weight * own_mask[:, None]

    def exchange(a):
        return lax.all_to_all(a, "blk", 0, 0, tiled=True, axis_index_groups=layers)

    def to_modes(a):
        turned = a.transpose(3, 1, 2, 0)
        return turned.reshape(outer, inner, modes, *turned.shape[1:]).swapaxes(0, 1)

    def to_samples(same, other):
        even = layer % 2 == 0
        parts = jnp.where(even, same, other), jnp.where(even, other, same)
        turned = jnp.stack(parts, axis=2).transpose(1, 2, 0, *range(3, 7))
        turned = turned.reshape(ranks * modes, *turned.shape[4:]).transpose(3, 1, 2, 0)
        return with_layout_constraint(turned, Layout((0, 1, 2, 3)))

    def send(a, step):
        return lax.ppermute(a, "blk", [(i, i ^ (step * inner)) for i in range(ranks)])

    def of_owner(a, step):
        return lax.dynamic_index_in_dim(a, layer ^ step, 1, keepdims=False)

    def mixed(odd, joint, x, g, ws):
        out = list(mix(place, odd, x, g, ws, jnp.bfloat16 if chans == 1 else F32, joint))
        if chans > 1:
            out[0] = lax.psum_scatter(out[0], "chan", scatter_dimension=5, tiled=True).astype(jnp.bfloat16)
        return [exchange(a) for a in out]

    def outward(x, g, ws, same):
        y, d = mixed(1, False, x, g, ws)
        spec_out = to_samples(same[0][:, 0] if chans == 1 else same[0], y)
        same, d, spec_out = lax.optimization_barrier((same, d, spec_out))
        return spec_out, to_samples(same[0][:, 1] if chans == 1 else same[1], d)

    barrier = lax.optimization_barrier
    place = layer.astype(jnp.int32).reshape(1)
    ready = lax.axis_index("blk") < ranks
    far, near = send(masked, 2), send(masked, 1)
    if chans > 1:
        cotangent = lax.all_gather(cotangent, "chan", axis=0, tiled=True)
    x, turned = stage(ready, lambda a, b: (exchange(to_modes(a)), to_modes(b)), spec_in, cotangent)
    g = exchange(turned)
    x, far, near = barrier((x, far, near))
    near_far = send(far, 1)
    x_parts = {step: of_owner(x, step) for step in (1, 2, 3)}
    pairs = {step: [send(x_parts[step], step)] for step in (2, 3)}
    g, near = barrier((g, near))
    g_parts = {step: of_owner(g, step) for step in (1, 2, 3)}
    for step in (2, 3):
        pairs[step].append(send(g_parts[step], step))
    same = stage(ready, functools.partial(mixed, 0, chans == 1), x, g, [masked, far])
    x_parts[1], g_parts[1], near_far, same = barrier((x_parts[1], g_parts[1], near_far, same))
    pairs[1] = [send(x_parts[1], 1), send(g_parts[1], 1)]
    spec_out, grad_in = stage(ready, outward, x, g, [near, near_far], same)
    spec_out, grad_in, pairs = barrier((spec_out, grad_in, pairs))
    grad_weight = weight_grad(place, x, g, [pairs[step] for step in (1, 2, 3)], own_mask)
    return spec_out, grad_in, grad_weight


def solution(mesh):
    in_specs = (
        P("chan", None, "blk", None),
        P("blk", None, "chan", None),
        P("blk", None, None),
        P("chan", None, "blk", None),
    )
    out_specs = (
        P("chan", None, "blk", None),
        P("chan", None, "blk", None),
        P("blk", None, "chan", None),
    )
    return jax.shard_map(local, mesh=mesh, in_specs=in_specs, out_specs=out_specs, check_vma=False)
```

```python
import functools

import jax
import jax.numpy as jnp
from jax import lax
from jax.experimental import pallas as pl
from jax.experimental.layout import Layout, with_layout_constraint
from jax.experimental.pallas import tpu as pltpu
from jax.sharding import PartitionSpec as P

F32 = jnp.float32
NN = (((1,), (0,)), ((), ()))
NT = (((1,), (1,)), ((), ()))
TN = (((0,), (0,)), ((), ()))


def dot(left, right, dims):
    return lax.dot_general(left, right, dims, preferred_element_type=F32)


def mix_kernel(layer_ref, x_ref, g_ref, same_ref, other_ref, *out_refs):
    inner, samples = x_ref.shape[0], x_ref.shape[4]
    y_ref, d_ref = out_refs if len(out_refs) == 2 else (out_refs[0].at[:, k] for k in range(2))

    def run(w_ref):
        def products(ref, j, dims):
            rows = ref[:, 0, j].reshape(inner * 2 * samples, ref.shape[-1])
            for c in range(2):
                yield dot(rows, w_ref[j, c], dims).reshape(inner, 2, samples, -1)

        for j in range(w_ref.shape[0]):
            real, imag = products(x_ref, j, NN)
            y_ref[:, 0, j, 0] = (real[:, 0] - imag[:, 1]).astype(y_ref.dtype)
            y_ref[:, 0, j, 1] = (real[:, 1] + imag[:, 0]).astype(y_ref.dtype)
            real, imag = products(g_ref, j, NT)
            d_ref[:, 0, j, 0] = (real[:, 0] + imag[:, 1]).astype(d_ref.dtype)
            d_ref[:, 0, j, 1] = (real[:, 1] - imag[:, 0]).astype(d_ref.dtype)

    for p, w_ref in enumerate((same_ref, other_ref)):
        pl.when(pl.program_id(0) == p)(functools.partial(run, w_ref))


def mix(layer, odd, x, g, ws, y_type, joint):
    inner, outer, modes, _, samples, _ = x.shape
    ci, co = ws[0].shape[2:]
    some = 2 if modes % 2 == 0 else 1

    def block(channels):
        return pl.BlockSpec(
            (inner, 1, some, 2, samples, channels), lambda p, k, layer: (0, layer[0] ^ (odd + 2 * p), k, 0, 0, 0)
        )

    def result(channels):
        return pl.BlockSpec((inner, 1, some, 2, samples, channels), lambda p, k, layer: (0, (layer[0] // 2) ^ p, k, 0, 0, 0))

    def weights(own):
        rest = 0 if own else modes // some - 1
        return pl.BlockSpec((some, 2, ci, co), lambda p, k, layer: (jnp.where(p == own, k, rest), 0, 0, 0))

    if joint:
        out_specs = [
            pl.BlockSpec((inner, 2, 1, some, 2, samples, co), lambda p, k, layer: (0, 0, (layer[0] // 2) ^ p, k, 0, 0, 0))
        ]
        out_shape = [jax.ShapeDtypeStruct((inner, 2, 2, modes, 2, samples, co), y_type)]
    else:
        out_specs = [result(co), result(ci)]
        out_shape = [
            jax.ShapeDtypeStruct((inner, 2, modes, 2, samples, co), y_type),
            jax.ShapeDtypeStruct((inner, 2, modes, 2, samples, ci), jnp.bfloat16),
        ]
    return pl.pallas_call(
        mix_kernel,
        grid_spec=pltpu.PrefetchScalarGridSpec(
            num_scalar_prefetch=1,
            grid=(2, modes // some),
            in_specs=[block(ci), block(co), weights(0), weights(1)],
            out_specs=out_specs,
        ),
        out_shape=out_shape,
        compiler_params=pltpu.CompilerParams(vmem_limit_bytes=40 * 1024 * 1024),
        name="mix",
    )(layer, x, g, *ws)


def gather_kernel(layer_ref, same_ref, other_ref, out_ref):
    def put(ref):
        out_ref[...] = ref[...].reshape(out_ref.shape)

    same = layer_ref[0] % 2 == pl.program_id(1)
    pl.when(same)(lambda: put(same_ref))
    pl.when(jnp.logical_not(same))(lambda: put(other_ref))


def gather(layer, same, kind, other):
    inner, _, modes, _, samples, channels = other.shape
    block = (inner, 1, modes, 2, samples, channels)
    if same.ndim == 7:
        same_spec = pl.BlockSpec((inner, 1, *block[1:]), lambda h, p, layer: (0, kind, h, 0, 0, 0, 0))
    else:
        same_spec = pl.BlockSpec(block, lambda h, p, layer: (0, h, 0, 0, 0, 0))
    return pl.pallas_call(
        gather_kernel,
        grid_spec=pltpu.PrefetchScalarGridSpec(
            num_scalar_prefetch=1,
            grid=(2, 2),
            in_specs=[same_spec, pl.BlockSpec(block, lambda h, p, layer: (0, h, 0, 0, 0, 0))],
            out_specs=pl.BlockSpec((1, inner, modes, 2, samples, channels), lambda h, p, layer: (2 * h + p, 0, 0, 0, 0, 0)),
        ),
        out_shape=jax.ShapeDtypeStruct((4, inner, modes, 2, samples, channels), other.dtype),
        compiler_params=pltpu.CompilerParams(vmem_limit_bytes=32 * 1024 * 1024),
        name="gather",
    )(layer, same, other)


def weight_grad_kernel(layer_ref, *refs):
    *pairs, mask_ref, out_ref = refs

    def rows(ref, c):
        return ref[..., c, :, :].reshape(-1, ref.shape[-1])

    x = jnp.concatenate([rows(ref, c) for ref in pairs[::2] for c in range(2)])
    g = [(rows(ref, 0), rows(ref, 1)) for ref in pairs[1::2]]
    mask = mask_ref[0].astype(F32)
    out_ref[0, 0] = dot(x, jnp.concatenate([part for real, imag in g for part in (real, imag)]), TN) * mask
    out_ref[0, 1] = dot(x, jnp.concatenate([part for real, imag in g for part in (imag, -real)]), TN) * mask


def weight_grad(layer, x, g, pairs, mask):
    inner, _, modes, _, samples, ci = x.shape
    co = g.shape[-1]

    def own(channels):
        return pl.BlockSpec((inner, 1, 1, 2, samples, channels), lambda j, layer: (0, layer[0], j, 0, 0, 0))

    def block(channels):
        return pl.BlockSpec((inner, 1, 2, samples, channels), lambda j, layer: (0, j, 0, 0, 0))

    return pl.pallas_call(
        weight_grad_kernel,
        grid_spec=pltpu.PrefetchScalarGridSpec(
            num_scalar_prefetch=1,
            grid=(modes,),
            in_specs=[own(ci), own(co), *[block(ci), block(co)] * len(pairs), pl.BlockSpec((1, ci, co), lambda j, layer: (j, 0, 0))],
            out_specs=pl.BlockSpec((1, 2, ci, co), lambda j, layer: (j, 0, 0, 0)),
        ),
        out_shape=jax.ShapeDtypeStruct((modes, 2, ci, co), F32),
        compiler_params=pltpu.CompilerParams(vmem_limit_bytes=40 * 1024 * 1024),
        name="weight_grad",
    )(layer, x, g, *(a for pair in pairs for a in pair), mask)


def stage(ready, work, *operands):
    shapes = jax.eval_shape(work, *operands)
    return lax.cond(ready, work, lambda *_: jax.tree.map(lambda a: jnp.zeros(a.shape, a.dtype), shapes), *operands)


def local(spec_in, weight, pattern, cotangent):
    ranks = lax.axis_size("blk")
    chans = lax.axis_size("chan")
    outer = 4
    inner = ranks // outer
    layer = lax.axis_index("blk") // inner
    layers = [[z * inner + r for r in range(inner)] for z in range(outer)]
    modes = weight.shape[0]
    in_rows, width = weight.shape[2:]
    block_size = width // pattern.shape[2]

    mask = jnp.repeat(jnp.repeat(pattern.astype(jnp.bfloat16), block_size, axis=1), block_size, axis=2)
    own_mask = lax.dynamic_slice_in_dim(mask, lax.axis_index("chan") * in_rows, in_rows, 1)
    masked = weight * own_mask[:, None]

    def exchange(a):
        return lax.all_to_all(a, "blk", 0, 0, tiled=True, axis_index_groups=layers)

    def to_modes(a):
        turned = a.transpose(3, 1, 2, 0)
        return turned.reshape(outer, inner, modes, *turned.shape[1:]).swapaxes(0, 1)

    def to_samples(same, kind, other):
        turned = gather(place, same, kind, other)
        turned = turned.reshape(ranks * modes, *turned.shape[3:]).transpose(3, 1, 2, 0)
        return with_layout_constraint(turned, Layout((0, 1, 2, 3)))

    def send(a, step):
        return lax.ppermute(a, "blk", [(i, i ^ (step * inner)) for i in range(ranks)])

    def of_owner(a, step):
        return lax.dynamic_index_in_dim(a, layer ^ step, 1, keepdims=False)

    def mixed(odd, joint, x, g, ws):
        out = list(mix(place, odd, x, g, ws, jnp.bfloat16 if chans == 1 else F32, joint))
        if chans > 1:
            out[0] = lax.psum_scatter(out[0], "chan", scatter_dimension=5, tiled=True).astype(jnp.bfloat16)
        return [exchange(a) for a in out]

    def outward(x, g, ws, same):
        y, d = mixed(1, False, x, g, ws)
        spec_out = to_samples(same[0], 0, y)
        same, d, spec_out = lax.optimization_barrier((same, d, spec_out))
        return spec_out, to_samples(same[-1], 1, d)

    barrier = lax.optimization_barrier
    place = layer.astype(jnp.int32).reshape(1)
    ready = lax.axis_index("blk") < ranks
    far, near = send(masked, 2), send(masked, 1)
    if chans > 1:
        cotangent = lax.all_gather(cotangent, "chan", axis=0, tiled=True)
    x, turned = stage(ready, lambda a, b: (exchange(to_modes(a)), to_modes(b)), spec_in, cotangent)
    g = exchange(turned)
    x, far, near = barrier((x, far, near))
    near_far = send(far, 1)
    x_parts = {step: of_owner(x, step) for step in (1, 2, 3)}
    pairs = {step: [send(x_parts[step], step)] for step in (2, 3)}
    g, near = barrier((g, near))
    g_parts = {step: of_owner(g, step) for step in (1, 2, 3)}
    for step in (2, 3):
        pairs[step].append(send(g_parts[step], step))
    same = stage(ready, functools.partial(mixed, 0, chans == 1), x, g, [masked, far])
    x_parts[1], g_parts[1], near_far, same = barrier((x_parts[1], g_parts[1], near_far, same))
    pairs[1] = [send(x_parts[1], 1), send(g_parts[1], 1)]
    spec_out, grad_in = stage(ready, outward, x, g, [near, near_far], same)
    spec_out, grad_in, pairs = barrier((spec_out, grad_in, pairs))
    grad_weight = weight_grad(place, x, g, [pairs[step] for step in (1, 2, 3)], own_mask)
    return spec_out, grad_in, grad_weight


def solution(mesh):
    in_specs = (
        P("chan", None, "blk", None),
        P("blk", None, "chan", None),
        P("blk", None, None),
        P("chan", None, "blk", None),
    )
    out_specs = (
        P("chan", None, "blk", None),
        P("chan", None, "blk", None),
        P("blk", None, "chan", None),
    )
    return jax.shard_map(local, mesh=mesh, in_specs=in_specs, out_specs=out_specs, check_vma=False)
```

```python
import functools

import jax
import jax.numpy as jnp
from jax import lax
from jax.experimental import pallas as pl
from jax.experimental.layout import Layout, with_layout_constraint
from jax.experimental.pallas import tpu as pltpu
from jax.sharding import PartitionSpec as P

F32 = jnp.float32
NN = (((1,), (0,)), ((), ()))
NT = (((1,), (1,)), ((), ()))
TN = (((0,), (0,)), ((), ()))


def dot(left, right, dims):
    return lax.dot_general(left, right, dims, preferred_element_type=F32)


def mix_kernel(layer_ref, x_ref, g_ref, same_ref, other_ref, *out_refs):
    inner, samples = x_ref.shape[0], x_ref.shape[4]
    y_ref, d_ref = out_refs if len(out_refs) == 2 else (out_refs[0].at[:, k] for k in range(2))

    def run(w_ref):
        def products(ref, j, dims):
            rows = ref[:, 0, j].reshape(inner * 2 * samples, ref.shape[-1])
            for c in range(2):
                yield dot(rows, w_ref[j, c], dims).reshape(inner, 2, samples, -1)

        for j in range(w_ref.shape[0]):
            real, imag = products(x_ref, j, NN)
            y_ref[:, 0, j, 0] = (real[:, 0] - imag[:, 1]).astype(y_ref.dtype)
            y_ref[:, 0, j, 1] = (real[:, 1] + imag[:, 0]).astype(y_ref.dtype)
            real, imag = products(g_ref, j, NT)
            d_ref[:, 0, j, 0] = (real[:, 0] + imag[:, 1]).astype(d_ref.dtype)
            d_ref[:, 0, j, 1] = (real[:, 1] - imag[:, 0]).astype(d_ref.dtype)

    for p, w_ref in enumerate((same_ref, other_ref)):
        pl.when(pl.program_id(0) == p)(functools.partial(run, w_ref))


def mix(layer, odd, x, g, ws, y_type, joint):
    inner, outer, modes, _, samples, _ = x.shape
    ci, co = ws[0].shape[2:]
    some = 2 if modes % 2 == 0 else 1

    def block(channels):
        return pl.BlockSpec(
            (inner, 1, some, 2, samples, channels), lambda p, k, layer: (0, layer[0] ^ (odd + 2 * p), k, 0, 0, 0)
        )

    def result(channels):
        return pl.BlockSpec((inner, 1, some, 2, samples, channels), lambda p, k, layer: (0, (layer[0] // 2) ^ p, k, 0, 0, 0))

    def weights(own):
        rest = 0 if own else modes // some - 1
        return pl.BlockSpec((some, 2, ci, co), lambda p, k, layer: (jnp.where(p == own, k, rest), 0, 0, 0))

    if joint:
        out_specs = [
            pl.BlockSpec((inner, 2, 1, some, 2, samples, co), lambda p, k, layer: (0, 0, (layer[0] // 2) ^ p, k, 0, 0, 0))
        ]
        out_shape = [jax.ShapeDtypeStruct((inner, 2, 2, modes, 2, samples, co), y_type)]
    else:
        out_specs = [result(co), result(ci)]
        out_shape = [
            jax.ShapeDtypeStruct((inner, 2, modes, 2, samples, co), y_type),
            jax.ShapeDtypeStruct((inner, 2, modes, 2, samples, ci), jnp.bfloat16),
        ]
    return pl.pallas_call(
        mix_kernel,
        grid_spec=pltpu.PrefetchScalarGridSpec(
            num_scalar_prefetch=1,
            grid=(2, modes // some),
            in_specs=[block(ci), block(co), weights(0), weights(1)],
            out_specs=out_specs,
        ),
        out_shape=out_shape,
        compiler_params=pltpu.CompilerParams(vmem_limit_bytes=40 * 1024 * 1024),
        name="mix",
    )(layer, x, g, *ws)


def gather_kernel(layer_ref, same_ref, other_ref, out_ref):
    def put(ref):
        out_ref[...] = ref[...].reshape(out_ref.shape)

    same = layer_ref[0] % 2 == pl.program_id(1)
    pl.when(same)(lambda: put(same_ref))
    pl.when(jnp.logical_not(same))(lambda: put(other_ref))


def gather(layer, same, kind, other):
    inner, modes, samples, channels = other.shape[0], other.shape[-4], *other.shape[-2:]

    def half(a):
        if a.ndim == 7:
            return pl.BlockSpec((inner, 1, 1, modes, 2, samples, channels), lambda h, p, layer: (0, kind, h, 0, 0, 0, 0))
        return pl.BlockSpec((inner, 1, modes, 2, samples, channels), lambda h, p, layer: (0, h, 0, 0, 0, 0))

    return pl.pallas_call(
        gather_kernel,
        grid_spec=pltpu.PrefetchScalarGridSpec(
            num_scalar_prefetch=1,
            grid=(2, 2),
            in_specs=[half(same), half(other)],
            out_specs=pl.BlockSpec((1, inner, modes, 2, samples, channels), lambda h, p, layer: (2 * h + p, 0, 0, 0, 0, 0)),
        ),
        out_shape=jax.ShapeDtypeStruct((4, inner, modes, 2, samples, channels), other.dtype),
        compiler_params=pltpu.CompilerParams(vmem_limit_bytes=32 * 1024 * 1024),
        name="gather",
    )(layer, same, other)


def weight_grad_kernel(layer_ref, *refs):
    *pairs, mask_ref, out_ref = refs

    def rows(ref, c):
        return ref[..., c, :, :].reshape(-1, ref.shape[-1])

    x = jnp.concatenate([rows(ref, c) for ref in pairs[::2] for c in range(2)])
    g = [(rows(ref, 0), rows(ref, 1)) for ref in pairs[1::2]]
    mask = mask_ref[0].astype(F32)
    out_ref[0, 0] = dot(x, jnp.concatenate([part for real, imag in g for part in (real, imag)]), TN) * mask
    out_ref[0, 1] = dot(x, jnp.concatenate([part for real, imag in g for part in (imag, -real)]), TN) * mask


def weight_grad(layer, x, g, pairs, mask):
    inner, _, modes, _, samples, ci = x.shape
    co = g.shape[-1]

    def own(channels):
        return pl.BlockSpec((inner, 1, 1, 2, samples, channels), lambda j, layer: (0, layer[0], j, 0, 0, 0))

    def block(channels):
        return pl.BlockSpec((inner, 1, 2, samples, channels), lambda j, layer: (0, j, 0, 0, 0))

    return pl.pallas_call(
        weight_grad_kernel,
        grid_spec=pltpu.PrefetchScalarGridSpec(
            num_scalar_prefetch=1,
            grid=(modes,),
            in_specs=[own(ci), own(co), *[block(ci), block(co)] * len(pairs), pl.BlockSpec((1, ci, co), lambda j, layer: (j, 0, 0))],
            out_specs=pl.BlockSpec((1, 2, ci, co), lambda j, layer: (j, 0, 0, 0)),
        ),
        out_shape=jax.ShapeDtypeStruct((modes, 2, ci, co), F32),
        compiler_params=pltpu.CompilerParams(vmem_limit_bytes=40 * 1024 * 1024),
        name="weight_grad",
    )(layer, x, g, *(a for pair in pairs for a in pair), mask)


def stage(ready, work, *operands):
    shapes = jax.eval_shape(work, *operands)
    return lax.cond(ready, work, lambda *_: jax.tree.map(lambda a: jnp.zeros(a.shape, a.dtype), shapes), *operands)


def local(spec_in, weight, pattern, cotangent):
    ranks = lax.axis_size("blk")
    chans = lax.axis_size("chan")
    outer = 4
    inner = ranks // outer
    layer = lax.axis_index("blk") // inner
    layers = [[z * inner + r for r in range(inner)] for z in range(outer)]
    modes = weight.shape[0]
    in_rows, width = weight.shape[2:]
    block_size = width // pattern.shape[2]

    mask = jnp.repeat(jnp.repeat(pattern.astype(jnp.bfloat16), block_size, axis=1), block_size, axis=2)
    own_mask = lax.dynamic_slice_in_dim(mask, lax.axis_index("chan") * in_rows, in_rows, 1)
    masked = weight * own_mask[:, None]

    def exchange(a):
        return lax.all_to_all(a, "blk", 0, 0, tiled=True, axis_index_groups=layers)

    def to_modes(a):
        turned = a.transpose(3, 1, 2, 0)
        return turned.reshape(outer, inner, modes, *turned.shape[1:]).swapaxes(0, 1)

    def to_samples(same, kind, other):
        turned = gather(place, same, kind, other)
        turned = turned.reshape(ranks * modes, *turned.shape[3:]).transpose(3, 1, 2, 0)
        return with_layout_constraint(turned, Layout((0, 1, 2, 3)))

    def send(a, step):
        return lax.ppermute(a, "blk", [(i, i ^ (step * inner)) for i in range(ranks)])

    def of_owner(a, step):
        return lax.dynamic_index_in_dim(a, layer ^ step, 1, keepdims=False)

    def mixed(odd, joint, x, g, ws):
        out = list(mix(place, odd, x, g, ws, jnp.bfloat16 if chans == 1 else F32, joint))
        if chans > 1:
            out[0] = lax.psum_scatter(out[0], "chan", scatter_dimension=5, tiled=True).astype(jnp.bfloat16)
        return [exchange(a) for a in out]

    def outward(x, g, ws, same):
        other = mixed(1, chans == 1, x, g, ws)
        return to_samples(same[0], 0, other[0]), to_samples(same[-1], 1, other[-1])

    barrier = lax.optimization_barrier
    place = layer.astype(jnp.int32).reshape(1)
    ready = lax.axis_index("blk") < ranks
    far, near = send(masked, 2), send(masked, 1)
    if chans > 1:
        cotangent = lax.all_gather(cotangent, "chan", axis=0, tiled=True)
    x, turned = stage(ready, lambda a, b: (exchange(to_modes(a)), to_modes(b)), spec_in, cotangent)
    g = exchange(turned)
    x, far, near = barrier((x, far, near))
    near_far = send(far, 1)
    x_parts = {step: of_owner(x, step) for step in (1, 2, 3)}
    pairs = {step: [send(x_parts[step], step)] for step in (2, 3)}
    g, near = barrier((g, near))
    g_parts = {step: of_owner(g, step) for step in (1, 2, 3)}
    for step in (2, 3):
        pairs[step].append(send(g_parts[step], step))
    same = stage(ready, functools.partial(mixed, 0, chans == 1), x, g, [masked, far])
    x_parts[1], g_parts[1], near_far, same = barrier((x_parts[1], g_parts[1], near_far, same))
    pairs[1] = [send(x_parts[1], 1), send(g_parts[1], 1)]
    spec_out, grad_in = stage(ready, outward, x, g, [near, near_far], same)
    spec_out, grad_in, pairs = barrier((spec_out, grad_in, pairs))
    grad_weight = weight_grad(place, x, g, [pairs[step] for step in (1, 2, 3)], own_mask)
    return spec_out, grad_in, grad_weight


def solution(mesh):
    in_specs = (
        P("chan", None, "blk", None),
        P("blk", None, "chan", None),
        P("blk", None, None),
        P("chan", None, "blk", None),
    )
    out_specs = (
        P("chan", None, "blk", None),
        P("chan", None, "blk", None),
        P("blk", None, "chan", None),
    )
    return jax.shard_map(local, mesh=mesh, in_specs=in_specs, out_specs=out_specs, check_vma=False)
```

```python
import functools

import jax
import jax.numpy as jnp
from jax import lax
from jax.experimental import pallas as pl
from jax.experimental.layout import Layout, with_layout_constraint
from jax.experimental.pallas import tpu as pltpu
from jax.sharding import PartitionSpec as P

F32 = jnp.float32
NN = (((1,), (0,)), ((), ()))
NT = (((1,), (1,)), ((), ()))
TN = (((0,), (0,)), ((), ()))


def dot(left, right, dims):
    return lax.dot_general(left, right, dims, preferred_element_type=F32)


def mix_kernel(layer_ref, x_ref, g_ref, same_ref, other_ref, *out_refs):
    inner, samples = x_ref.shape[0], x_ref.shape[4]
    y_ref, d_ref = out_refs if len(out_refs) == 2 else (out_refs[0].at[:, k] for k in range(2))

    def run(w_ref):
        def products(ref, j, dims):
            rows = ref[:, 0, j].reshape(inner * 2 * samples, ref.shape[-1])
            for c in range(2):
                yield dot(rows, w_ref[j, c], dims).reshape(inner, 2, samples, -1)

        for j in range(w_ref.shape[0]):
            real, imag = products(x_ref, j, NN)
            y_ref[:, 0, j, 0] = (real[:, 0] - imag[:, 1]).astype(y_ref.dtype)
            y_ref[:, 0, j, 1] = (real[:, 1] + imag[:, 0]).astype(y_ref.dtype)
            real, imag = products(g_ref, j, NT)
            d_ref[:, 0, j, 0] = (real[:, 0] + imag[:, 1]).astype(d_ref.dtype)
            d_ref[:, 0, j, 1] = (real[:, 1] - imag[:, 0]).astype(d_ref.dtype)

    for p, w_ref in enumerate((same_ref, other_ref)):
        pl.when(pl.program_id(0) == p)(functools.partial(run, w_ref))


def mix(layer, odd, x, g, ws, y_type, joint):
    inner, outer, modes, _, samples, _ = x.shape
    ci, co = ws[0].shape[2:]
    some = modes

    def block(channels):
        return pl.BlockSpec(
            (inner, 1, some, 2, samples, channels), lambda p, k, layer: (0, layer[0] ^ (odd + 2 * p), k, 0, 0, 0)
        )

    def result(channels):
        return pl.BlockSpec((inner, 1, some, 2, samples, channels), lambda p, k, layer: (0, (layer[0] // 2) ^ p, k, 0, 0, 0))

    def weights(own):
        rest = 0 if own else modes // some - 1
        return pl.BlockSpec((some, 2, ci, co), lambda p, k, layer: (jnp.where(p == own, k, rest), 0, 0, 0))

    if joint:
        out_specs = [
            pl.BlockSpec((inner, 2, 1, some, 2, samples, co), lambda p, k, layer: (0, 0, (layer[0] // 2) ^ p, k, 0, 0, 0))
        ]
        out_shape = [jax.ShapeDtypeStruct((inner, 2, 2, modes, 2, samples, co), y_type)]
    else:
        out_specs = [result(co), result(ci)]
        out_shape = [
            jax.ShapeDtypeStruct((inner, 2, modes, 2, samples, co), y_type),
            jax.ShapeDtypeStruct((inner, 2, modes, 2, samples, ci), jnp.bfloat16),
        ]
    return pl.pallas_call(
        mix_kernel,
        grid_spec=pltpu.PrefetchScalarGridSpec(
            num_scalar_prefetch=1,
            grid=(2, modes // some),
            in_specs=[block(ci), block(co), weights(0), weights(1)],
            out_specs=out_specs,
        ),
        out_shape=out_shape,
        compiler_params=pltpu.CompilerParams(vmem_limit_bytes=48 * 1024 * 1024),
        name="mix",
    )(layer, x, g, *ws)


def gather_kernel(layer_ref, same_ref, other_ref, out_ref):
    def put(ref):
        out_ref[...] = ref[...].reshape(out_ref.shape)

    same = layer_ref[0] % 2 == pl.program_id(1)
    pl.when(same)(lambda: put(same_ref))
    pl.when(jnp.logical_not(same))(lambda: put(other_ref))


def gather(layer, same, kind, other):
    inner, modes, samples, channels = other.shape[0], other.shape[-4], *other.shape[-2:]

    def half(a):
        if a.ndim == 7:
            return pl.BlockSpec((inner, 1, 1, modes, 2, samples, channels), lambda h, p, layer: (0, kind, h, 0, 0, 0, 0))
        return pl.BlockSpec((inner, 1, modes, 2, samples, channels), lambda h, p, layer: (0, h, 0, 0, 0, 0))

    return pl.pallas_call(
        gather_kernel,
        grid_spec=pltpu.PrefetchScalarGridSpec(
            num_scalar_prefetch=1,
            grid=(2, 2),
            in_specs=[half(same), half(other)],
            out_specs=pl.BlockSpec((1, inner, modes, 2, samples, channels), lambda h, p, layer: (2 * h + p, 0, 0, 0, 0, 0)),
        ),
        out_shape=jax.ShapeDtypeStruct((4, inner, modes, 2, samples, channels), other.dtype),
        compiler_params=pltpu.CompilerParams(vmem_limit_bytes=32 * 1024 * 1024),
        name="gather",
    )(layer, same, other)


def weight_grad_kernel(layer_ref, *refs):
    *pairs, mask_ref, out_ref = refs

    def rows(ref, c):
        return ref[..., c, :, :].reshape(-1, ref.shape[-1])

    x = jnp.concatenate([rows(ref, c) for ref in pairs[::2] for c in range(2)])
    g = [(rows(ref, 0), rows(ref, 1)) for ref in pairs[1::2]]
    mask = mask_ref[0].astype(F32)
    out_ref[0, 0] = dot(x, jnp.concatenate([part for real, imag in g for part in (real, imag)]), TN) * mask
    out_ref[0, 1] = dot(x, jnp.concatenate([part for real, imag in g for part in (imag, -real)]), TN) * mask


def weight_grad(layer, x, g, pairs, mask):
    inner, _, modes, _, samples, ci = x.shape
    co = g.shape[-1]

    def own(channels):
        return pl.BlockSpec((inner, 1, 1, 2, samples, channels), lambda j, layer: (0, layer[0], j, 0, 0, 0))

    def block(channels):
        return pl.BlockSpec((inner, 1, 2, samples, channels), lambda j, layer: (0, j, 0, 0, 0))

    return pl.pallas_call(
        weight_grad_kernel,
        grid_spec=pltpu.PrefetchScalarGridSpec(
            num_scalar_prefetch=1,
            grid=(modes,),
            in_specs=[own(ci), own(co), *[block(ci), block(co)] * len(pairs), pl.BlockSpec((1, ci, co), lambda j, layer: (j, 0, 0))],
            out_specs=pl.BlockSpec((1, 2, ci, co), lambda j, layer: (j, 0, 0, 0)),
        ),
        out_shape=jax.ShapeDtypeStruct((modes, 2, ci, co), F32),
        compiler_params=pltpu.CompilerParams(vmem_limit_bytes=40 * 1024 * 1024),
        name="weight_grad",
    )(layer, x, g, *(a for pair in pairs for a in pair), mask)


def stage(ready, work, *operands):
    shapes = jax.eval_shape(work, *operands)
    return lax.cond(ready, work, lambda *_: jax.tree.map(lambda a: jnp.zeros(a.shape, a.dtype), shapes), *operands)


def local(spec_in, weight, pattern, cotangent):
    ranks = lax.axis_size("blk")
    chans = lax.axis_size("chan")
    outer = 4
    inner = ranks // outer
    layer = lax.axis_index("blk") // inner
    layers = [[z * inner + r for r in range(inner)] for z in range(outer)]
    modes = weight.shape[0]
    in_rows, width = weight.shape[2:]
    block_size = width // pattern.shape[2]

    mask = jnp.repeat(jnp.repeat(pattern.astype(jnp.bfloat16), block_size, axis=1), block_size, axis=2)
    own_mask = lax.dynamic_slice_in_dim(mask, lax.axis_index("chan") * in_rows, in_rows, 1)
    masked = weight * own_mask[:, None]

    def exchange(a):
        return lax.all_to_all(a, "blk", 0, 0, tiled=True, axis_index_groups=layers)

    def to_modes(a):
        turned = a.transpose(3, 1, 2, 0)
        return turned.reshape(outer, inner, modes, *turned.shape[1:]).swapaxes(0, 1)

    def to_samples(same, kind, other):
        turned = gather(place, same, kind, other)
        turned = turned.reshape(ranks * modes, *turned.shape[3:]).transpose(3, 1, 2, 0)
        return with_layout_constraint(turned, Layout((0, 1, 2, 3)))

    def send(a, step):
        return lax.ppermute(a, "blk", [(i, i ^ (step * inner)) for i in range(ranks)])

    def of_owner(a, step):
        return lax.dynamic_index_in_dim(a, layer ^ step, 1, keepdims=False)

    def mixed(odd, joint, x, g, ws):
        out = list(mix(place, odd, x, g, ws, jnp.bfloat16 if chans == 1 else F32, joint))
        if chans > 1:
            out[0] = lax.psum_scatter(out[0], "chan", scatter_dimension=5, tiled=True).astype(jnp.bfloat16)
        return [exchange(a) for a in out]

    def outward(x, g, ws, same):
        other = mixed(1, chans == 1, x, g, ws)
        return to_samples(same[0], 0, other[0]), to_samples(same[-1], 1, other[-1])

    barrier = lax.optimization_barrier
    place = layer.astype(jnp.int32).reshape(1)
    ready = lax.axis_index("blk") < ranks
    far, near = send(masked, 2), send(masked, 1)
    if chans > 1:
        cotangent = lax.all_gather(cotangent, "chan", axis=0, tiled=True)
    x, turned = stage(ready, lambda a, b: (exchange(to_modes(a)), to_modes(b)), spec_in, cotangent)
    g = exchange(turned)
    x, far, near = barrier((x, far, near))
    near_far = send(far, 1)
    x_parts = {step: of_owner(x, step) for step in (1, 2, 3)}
    pairs = {step: [send(x_parts[step], step)] for step in (2, 3)}
    g, near = barrier((g, near))
    g_parts = {step: of_owner(g, step) for step in (1, 2, 3)}
    for step in (2, 3):
        pairs[step].append(send(g_parts[step], step))
    same = stage(ready, functools.partial(mixed, 0, chans == 1), x, g, [masked, far])
    x_parts[1], g_parts[1], near_far, same = barrier((x_parts[1], g_parts[1], near_far, same))
    pairs[1] = [send(x_parts[1], 1), send(g_parts[1], 1)]
    spec_out, grad_in = stage(ready, outward, x, g, [near, near_far], same)
    spec_out, grad_in, pairs = barrier((spec_out, grad_in, pairs))
    grad_weight = weight_grad(place, x, g, [pairs[step] for step in (1, 2, 3)], own_mask)
    return spec_out, grad_in, grad_weight


def solution(mesh):
    in_specs = (
        P("chan", None, "blk", None),
        P("blk", None, "chan", None),
        P("blk", None, None),
        P("chan", None, "blk", None),
    )
    out_specs = (
        P("chan", None, "blk", None),
        P("chan", None, "blk", None),
        P("blk", None, "chan", None),
    )
    return jax.shard_map(local, mesh=mesh, in_specs=in_specs, out_specs=out_specs, check_vma=False)
```

```python
import functools

import jax
import jax.numpy as jnp
from jax import lax
from jax.experimental import pallas as pl
from jax.experimental.layout import Layout, with_layout_constraint
from jax.experimental.pallas import tpu as pltpu
from jax.sharding import PartitionSpec as P

F32 = jnp.float32
NN = (((1,), (0,)), ((), ()))
NT = (((1,), (1,)), ((), ()))
TN = (((0,), (0,)), ((), ()))


def dot(left, right, dims):
    return lax.dot_general(left, right, dims, preferred_element_type=F32)


def mix_kernel(layer_ref, x_ref, g_ref, same_ref, other_ref, *out_refs):
    inner, samples = x_ref.shape[0], x_ref.shape[4]
    y_ref, d_ref = out_refs if len(out_refs) == 2 else (out_refs[0].at[:, k] for k in range(2))

    def run(w_ref):
        def products(ref, j, dims):
            rows = ref[:, 0, j].reshape(inner * 2 * samples, ref.shape[-1])
            for c in range(2):
                yield dot(rows, w_ref[j, c], dims).reshape(inner, 2, samples, -1)

        for j in range(w_ref.shape[0]):
            real, imag = products(x_ref, j, NN)
            y_ref[:, 0, j, 0] = (real[:, 0] - imag[:, 1]).astype(y_ref.dtype)
            y_ref[:, 0, j, 1] = (real[:, 1] + imag[:, 0]).astype(y_ref.dtype)
            real, imag = products(g_ref, j, NT)
            d_ref[:, 0, j, 0] = (real[:, 0] + imag[:, 1]).astype(d_ref.dtype)
            d_ref[:, 0, j, 1] = (real[:, 1] - imag[:, 0]).astype(d_ref.dtype)

    for p, w_ref in enumerate((same_ref, other_ref)):
        pl.when(pl.program_id(0) == p)(functools.partial(run, w_ref))


def mix(layer, odd, x, g, ws, y_type, joint):
    inner, outer, modes, _, samples, _ = x.shape
    ci, co = ws[0].shape[2:]
    some = modes

    def block(channels):
        return pl.BlockSpec(
            (inner, 1, some, 2, samples, channels), lambda p, k, layer: (0, layer[0] ^ (odd + 2 * p), k, 0, 0, 0)
        )

    def result(channels):
        return pl.BlockSpec((inner, 1, some, 2, samples, channels), lambda p, k, layer: (0, (layer[0] // 2) ^ p, k, 0, 0, 0))

    def weights(own):
        rest = 0 if own else modes // some - 1
        return pl.BlockSpec((some, 2, ci, co), lambda p, k, layer: (jnp.where(p == own, k, rest), 0, 0, 0))

    if joint:
        out_specs = [
            pl.BlockSpec((inner, 2, 1, some, 2, samples, co), lambda p, k, layer: (0, 0, (layer[0] // 2) ^ p, k, 0, 0, 0))
        ]
        out_shape = [jax.ShapeDtypeStruct((inner, 2, 2, modes, 2, samples, co), y_type)]
    else:
        out_specs = [result(co), result(ci)]
        out_shape = [
            jax.ShapeDtypeStruct((inner, 2, modes, 2, samples, co), y_type),
            jax.ShapeDtypeStruct((inner, 2, modes, 2, samples, ci), jnp.bfloat16),
        ]
    return pl.pallas_call(
        mix_kernel,
        grid_spec=pltpu.PrefetchScalarGridSpec(
            num_scalar_prefetch=1,
            grid=(2, modes // some),
            in_specs=[block(ci), block(co), weights(0), weights(1)],
            out_specs=out_specs,
        ),
        out_shape=out_shape,
        compiler_params=pltpu.CompilerParams(vmem_limit_bytes=48 * 1024 * 1024),
        name="mix",
    )(layer, x, g, *ws)


def gather_kernel(layer_ref, same_ref, other_ref, out_ref):
    def put(ref):
        out_ref[...] = ref[...].reshape(out_ref.shape)

    same = layer_ref[0] % 2 == pl.program_id(1)
    pl.when(same)(lambda: put(same_ref))
    pl.when(jnp.logical_not(same))(lambda: put(other_ref))


def gather(layer, same, kind, other):
    inner, modes, samples, channels = other.shape[0], other.shape[-4], *other.shape[-2:]

    def half(a):
        if a.ndim == 7:
            return pl.BlockSpec((inner, 1, 1, modes, 2, samples, channels), lambda h, p, layer: (0, kind, h, 0, 0, 0, 0))
        return pl.BlockSpec((inner, 1, modes, 2, samples, channels), lambda h, p, layer: (0, h, 0, 0, 0, 0))

    return pl.pallas_call(
        gather_kernel,
        grid_spec=pltpu.PrefetchScalarGridSpec(
            num_scalar_prefetch=1,
            grid=(2, 2),
            in_specs=[half(same), half(other)],
            out_specs=pl.BlockSpec((1, inner, modes, 2, samples, channels), lambda h, p, layer: (2 * h + p, 0, 0, 0, 0, 0)),
        ),
        out_shape=jax.ShapeDtypeStruct((4, inner, modes, 2, samples, channels), other.dtype),
        compiler_params=pltpu.CompilerParams(vmem_limit_bytes=32 * 1024 * 1024),
        name="gather",
    )(layer, same, other)


def weight_grad_kernel(layer_ref, *refs):
    *pairs, mask_ref, out_ref = refs

    def rows(ref, j, c):
        return ref[..., j, c, :, :].reshape(-1, ref.shape[-1])

    for j in range(out_ref.shape[0]):
        x = jnp.concatenate([rows(ref, j, c) for ref in pairs[::2] for c in range(2)])
        g = [(rows(ref, j, 0), rows(ref, j, 1)) for ref in pairs[1::2]]
        mask = mask_ref[j].astype(F32)
        out_ref[j, 0] = dot(x, jnp.concatenate([part for real, imag in g for part in (real, imag)]), TN) * mask
        out_ref[j, 1] = dot(x, jnp.concatenate([part for real, imag in g for part in (imag, -real)]), TN) * mask


def weight_grad(layer, x, g, pairs, mask):
    inner, _, modes, _, samples, ci = x.shape
    co = g.shape[-1]
    some = 2 if modes % 2 == 0 else 1

    def own(channels):
        return pl.BlockSpec((inner, 1, some, 2, samples, channels), lambda j, layer: (0, layer[0], j, 0, 0, 0))

    def block(channels):
        return pl.BlockSpec((inner, some, 2, samples, channels), lambda j, layer: (0, j, 0, 0, 0))

    return pl.pallas_call(
        weight_grad_kernel,
        grid_spec=pltpu.PrefetchScalarGridSpec(
            num_scalar_prefetch=1,
            grid=(modes // some,),
            in_specs=[own(ci), own(co), *[block(ci), block(co)] * len(pairs), pl.BlockSpec((some, ci, co), lambda j, layer: (j, 0, 0))],
            out_specs=pl.BlockSpec((some, 2, ci, co), lambda j, layer: (j, 0, 0, 0)),
        ),
        out_shape=jax.ShapeDtypeStruct((modes, 2, ci, co), F32),
        compiler_params=pltpu.CompilerParams(vmem_limit_bytes=40 * 1024 * 1024),
        name="weight_grad",
    )(layer, x, g, *(a for pair in pairs for a in pair), mask)


def stage(ready, work, *operands):
    shapes = jax.eval_shape(work, *operands)
    return lax.cond(ready, work, lambda *_: jax.tree.map(lambda a: jnp.zeros(a.shape, a.dtype), shapes), *operands)


def local(spec_in, weight, pattern, cotangent):
    ranks = lax.axis_size("blk")
    chans = lax.axis_size("chan")
    outer = 4
    inner = ranks // outer
    layer = lax.axis_index("blk") // inner
    layers = [[z * inner + r for r in range(inner)] for z in range(outer)]
    modes = weight.shape[0]
    in_rows, width = weight.shape[2:]
    block_size = width // pattern.shape[2]

    mask = jnp.repeat(jnp.repeat(pattern.astype(jnp.bfloat16), block_size, axis=1), block_size, axis=2)
    own_mask = lax.dynamic_slice_in_dim(mask, lax.axis_index("chan") * in_rows, in_rows, 1)
    masked = weight * own_mask[:, None]

    def exchange(a):
        return lax.all_to_all(a, "blk", 0, 0, tiled=True, axis_index_groups=layers)

    def to_modes(a):
        turned = a.transpose(3, 1, 2, 0)
        return turned.reshape(outer, inner, modes, *turned.shape[1:]).swapaxes(0, 1)

    def to_samples(same, kind, other):
        turned = gather(place, same, kind, other)
        turned = turned.reshape(ranks * modes, *turned.shape[3:]).transpose(3, 1, 2, 0)
        return with_layout_constraint(turned, Layout((0, 1, 2, 3)))

    def send(a, step):
        return lax.ppermute(a, "blk", [(i, i ^ (step * inner)) for i in range(ranks)])

    def of_owner(a, step):
        return lax.dynamic_index_in_dim(a, layer ^ step, 1, keepdims=False)

    def mixed(odd, joint, x, g, ws):
        out = list(mix(place, odd, x, g, ws, jnp.bfloat16 if chans == 1 else F32, joint))
        if chans > 1:
            out[0] = lax.psum_scatter(out[0], "chan", scatter_dimension=5, tiled=True).astype(jnp.bfloat16)
        return [exchange(a) for a in out]

    def outward(x, g, ws, same):
        other = mixed(1, chans == 1, x, g, ws)
        return to_samples(same[0], 0, other[0]), to_samples(same[-1], 1, other[-1])

    barrier = lax.optimization_barrier
    place = layer.astype(jnp.int32).reshape(1)
    ready = lax.axis_index("blk") < ranks
    far, near = send(masked, 2), send(masked, 1)
    if chans > 1:
        cotangent = lax.all_gather(cotangent, "chan", axis=0, tiled=True)
    x, turned = stage(ready, lambda a, b: (exchange(to_modes(a)), to_modes(b)), spec_in, cotangent)
    g = exchange(turned)
    x, far, near = barrier((x, far, near))
    near_far = send(far, 1)
    x_parts = {step: of_owner(x, step) for step in (1, 2, 3)}
    pairs = {step: [send(x_parts[step], step)] for step in (2, 3)}
    g, near = barrier((g, near))
    g_parts = {step: of_owner(g, step) for step in (1, 2, 3)}
    for step in (2, 3):
        pairs[step].append(send(g_parts[step], step))
    same = stage(ready, functools.partial(mixed, 0, chans == 1), x, g, [masked, far])
    x_parts[1], g_parts[1], near_far, same = barrier((x_parts[1], g_parts[1], near_far, same))
    pairs[1] = [send(x_parts[1], 1), send(g_parts[1], 1)]
    spec_out, grad_in = stage(ready, outward, x, g, [near, near_far], same)
    spec_out, grad_in, pairs = barrier((spec_out, grad_in, pairs))
    grad_weight = weight_grad(place, x, g, [pairs[step] for step in (1, 2, 3)], own_mask)
    return spec_out, grad_in, grad_weight


def solution(mesh):
    in_specs = (
        P("chan", None, "blk", None),
        P("blk", None, "chan", None),
        P("blk", None, None),
        P("chan", None, "blk", None),
    )
    out_specs = (
        P("chan", None, "blk", None),
        P("chan", None, "blk", None),
        P("blk", None, "chan", None),
    )
    return jax.shard_map(local, mesh=mesh, in_specs=in_specs, out_specs=out_specs, check_vma=False)
```
